32 devices in a mesh: ctx: 4 (over x, core), tp: 4 (over z), pp: 2 (over y).
Axes of the slice: x: 2, y: 2, z: 4, core: 2. Of those that a mesh axis runs over, the one named last changes fastest.
Arguments:
- queries: bfloat16 [2, 512, 8192], P('pp', 'ctx', 'tp'), may hold values from -6 to 6
- key_feats: bfloat16 [2, 512, 8192], P('pp', 'ctx', 'tp'), may hold values from -6 to 6
- value_feats: bfloat16 [2, 512, 8192], P('pp', 'ctx', 'tp'), may hold values from -6 to 6
- cotangent: bfloat16 [2, 512, 8192], P('pp', 'ctx', 'tp'), may hold values from -70 to 70
- filters: float32 [2, 512, 128], P('pp', 'tp'), may hold values from -0.5 to 0.5
Outputs:
- grad_queries: bfloat16 [2, 512, 8192], P('pp', 'ctx', 'tp')
- grad_keys: bfloat16 [2, 512, 8192], P('pp', 'ctx', 'tp')
- handed: bfloat16 [2, 512, 8192], P('pp', 'ctx', 'tp')
- grad_filters: float32 [2, 512, 128], P('pp', 'tp')
The draws below stay inside these ranges and needn't reach their ends.
All inputs are finite; a program needn't handle non-finite values.
Results may differ from the reference program's by a relative error of at most 0.0058.
Values may be sent and summed in bfloat16 or wider, within the bound.
A program may use at most 64 MiB of HBM per device.

```python
import math
import jax
import jax.numpy as jnp
from jax import lax

D = 8192
TAPS = 128
GROUP = 16
GROUPS = 512
TOKENS = 512
N_PP = 2


def draw_cotangent(key, part):
    keys = jax.random.split(key, 3)
    token_pos = jnp.arange(TOKENS, dtype=jnp.float32) / TOKENS
    channel_pos = jnp.arange(D, dtype=jnp.float32) / D
    col_scale = 10.0 ** (0.5 * channel_pos + 0.5 * jax.random.uniform(keys[2], (D,), jnp.float32))
    base = jnp.clip(jax.random.normal(keys[0], (N_PP, TOKENS, D), jnp.float32), -6.0, 6.0)
    row_scale = 10.0 ** (0.5 * token_pos + 0.5 * jax.random.uniform(keys[1], (TOKENS,), jnp.float32))
    values = base * row_scale[None, :, None] * col_scale[None, None, :] / 10.0
    return values.astype(jnp.bfloat16)


def levels(rng, shape, cuts, least, high):
    loudness = 1.0
    for dim, blocks in cuts:
        heights = jax.random.uniform(jax.random.fold_in(jax.random.fold_in(rng, 6), dim), (blocks,), jnp.float32, least / len(cuts), high / len(cuts))
        loudness = loudness * jnp.repeat(jnp.exp(heights), shape[dim] // blocks).reshape((-1,) + (1,) * (len(shape) - 1 - dim))
    return loudness


def scatter_about(own_key, extent, deviation, most, cuts=(), kind=jnp.bfloat16):
    values = jax.random.normal(own_key, extent, jnp.float32) * deviation
    if len(cuts) > 0:
        values = levels(own_key, extent, cuts, -0.22, 0.18) * values
    return jnp.clip(values, min=-most, max=most).astype(kind)


def setup_inputs(seed: int = 0) -> dict:
    key_list = jax.random.split(jax.random.key(seed), 6)
    queries = scatter_about(key_list[0], (N_PP, TOKENS, D), 1.0, 6.0, ((0, 2), (1, 4), (2, 4)))
    key_feats = scatter_about(key_list[1], (N_PP, TOKENS, D), 1.0, 6.0, ((0, 2), (1, 4), (2, 4)))
    value_feats = scatter_about(key_list[2], (N_PP, TOKENS, D), 1.0, 6.0, ((0, 2), (1, 4), (2, 4)))
    cotangent = draw_cotangent(jax.random.fold_in(key_list[5], 71), 0)
    filters = scatter_about(key_list[4], (N_PP, GROUPS, TAPS), TAPS ** -0.5, 0.5, ((0, 2), (1, 4)), jnp.float32)
    return dict(queries=queries, key_feats=key_feats, value_feats=value_feats, cotangent=cotangent, filters=filters)


def column_block(queries, key_feats, value_feats, cotangent, taps_bf):
    channels = queries.shape[1]
    per_channel = jnp.repeat(taps_bf.astype(jnp.float32), GROUP, axis=0).T
    product = (key_feats.astype(jnp.float32) * value_feats.astype(jnp.float32)).astype(jnp.bfloat16)
    product_f = product.astype(jnp.float32)
    zero_rim = jnp.zeros((TAPS - 1, channels), jnp.float32)
    padded_front = jnp.concatenate([zero_rim, product_f], axis=0)

    def fwd_step(tap_index, running):
        return running + per_channel[tap_index] * lax.dynamic_slice_in_dim(padded_front, TAPS - 1 - tap_index, TOKENS, 0)
    mixed = lax.fori_loop(0, TAPS, fwd_step, jnp.zeros((TOKENS, channels), jnp.float32))
    grad_q = (cotangent.astype(jnp.float32) * mixed).astype(jnp.bfloat16)
    weighted = (cotangent.astype(jnp.float32) * queries.astype(jnp.float32)).astype(jnp.bfloat16)
    weighted_f = weighted.astype(jnp.float32)
    padded_back = jnp.concatenate([weighted_f, zero_rim], axis=0)

    def back_step(tap_index, running):
        return running + per_channel[tap_index] * lax.dynamic_slice_in_dim(padded_back, tap_index, TOKENS, 0)
    dproduct = lax.fori_loop(0, TAPS, back_step, jnp.zeros((TOKENS, channels), jnp.float32))
    grad_k = (dproduct * value_feats.astype(jnp.float32)).astype(jnp.bfloat16)
    dvalues = (dproduct * key_feats.astype(jnp.float32)).astype(jnp.bfloat16)

    def tap_sum(tap_index):
        return lax.optimization_barrier(jnp.sum(weighted_f * lax.dynamic_slice_in_dim(padded_front, TAPS - 1 - tap_index, TOKENS, 0), axis=0))
    per_tap = lax.map(tap_sum, jnp.arange(TAPS))
    raw_grad = per_tap.reshape(TAPS, channels // GROUP, GROUP).sum(axis=2).T
    return (grad_q, grad_k, dvalues, raw_grad)

def reference(queries, key_feats, value_feats, cotangent, filters):
    channels = min(D, 512)
    num_blocks = D // channels

    def split(array):
        return array.reshape(TOKENS, num_blocks, channels).transpose(1, 0, 2)

    def merge(array):
        return array.transpose(1, 0, 2).reshape(TOKENS, D)
    grads_q = []
    grads_k = []
    values_all = []
    raw_all = []
    for section in range(N_PP):
        taps_bf = filters[section].astype(jnp.bfloat16).reshape(num_blocks, channels // GROUP, TAPS)
        results = lax.map(lambda pieces: column_block(*pieces), (split(queries[section]), split(key_feats[section]), split(value_feats[section]), split(cotangent[section]), taps_bf))
        grads_q.append(merge(results[0]))
        grads_k.append(merge(results[1]))
        values_all.append(merge(results[2]))
        raw_all.append(results[3].reshape(GROUPS, TAPS))
    grad_queries = jnp.stack(grads_q)
    grad_keys = jnp.stack(grads_k)
    dvalues = jnp.stack(values_all)
    handed = jnp.concatenate([dvalues[1:], jnp.zeros_like(dvalues[:1])], axis=0)
    raw_grad = jnp.stack(raw_all)
    total_norm = jnp.sqrt(jnp.sum(raw_grad * raw_grad))
    clip_level = 0.25 * math.sqrt(N_PP * GROUPS * TAPS)
    factor = jnp.minimum(1.0, clip_level / (total_norm + 1e-06))
    grad_filters = raw_grad * factor
    return (grad_queries, grad_keys, handed, grad_filters)
```

```python
import functools
import math

import jax
import jax.numpy as jnp
from jax import lax
from jax.experimental import pallas as pl
from jax.experimental.pallas import tpu as pltpu
from jax.sharding import PartitionSpec as P

TAPS = 128
GROUP = 16
LANES = 128
PER = LANES // GROUP
BLK = 32
WIDTH = 256
MESH = pl.DeviceIdType.MESH
F32 = jnp.float32
BF16 = jnp.bfloat16


def dot(lhs, rhs, contract):
    return lax.dot_general(lhs, rhs, (contract, ((), ())), preferred_element_type=F32)


def kernel(
    sizes, chunk, clip_level,
    q_hbm, k_hbm, v_hbm, c_hbm, f_ref,
    gq_hbm, gk_hbm, ho_hbm, gf_ref,
    qv, kv, vv, cv, wext, pext, gq, gk, dv, toep_b, toep_f, taps, raws, norms,
    in_sem, out_sem, w_send, w_recv, p_send, p_recv, d_send, d_recv,
    r_send, r_recv, n_send, n_recv,
):
    n_ctx, n_tp, n_pp = sizes
    ctx, tp, pp = (lax.axis_index(a) for a in ("ctx", "tp", "pp"))
    n_chunks, rows, _ = qv.shape
    groups = f_ref.shape[1]
    n_quad = n_tp * n_pp
    me = pp * n_tp + tp
    has_next, has_prev = ctx < n_ctx - 1, ctx > 0
    span = BLK + TAPS
    blocks = rows // BLK
    subs = chunk // LANES

    def each(count, body):
        def step(i, _):
            body(i)
            return 0
        lax.fori_loop(0, count, step, 0)

    def ctx_peer(d):
        return {"ctx": lax.rem(ctx + d, n_ctx)}

    def quad(d):
        other = lax.rem(me + d, n_quad)
        return {"tp": lax.rem(other, n_tp), "pp": other // n_tp}

    barrier = pltpu.get_barrier_semaphore()
    each(n_ctx - 1, lambda d: pl.semaphore_signal(
        barrier, inc=1, device_id=ctx_peer(d + 1), device_id_type=MESH))
    each(n_quad - 1, lambda d: pl.semaphore_signal(
        barrier, inc=1, device_id=quad(d + 1), device_id_type=MESH))

    def load(which, hbm, vmem, i):
        cols = pl.ds(pl.multiple_of(i * chunk, chunk), chunk)
        return pltpu.make_async_copy(hbm.at[0, :, cols], vmem.at[i], in_sem.at[which, i])

    def store(which, vmem, hbm, i):
        cols = pl.ds(pl.multiple_of(i * chunk, chunk), chunk)
        return pltpu.make_async_copy(vmem.at[i], hbm.at[0, :, cols], out_sem.at[which, i])

    loads = ((c_hbm, cv), (q_hbm, qv), (k_hbm, kv), (v_hbm, vv))

    def start_loads(i):
        for which, (hbm, vmem) in enumerate(loads):
            load(which, hbm, vmem, i).start()
    each(n_chunks, start_loads)

    rounded = f_ref[0].astype(BF16)
    flip = (
        lax.broadcasted_iota(jnp.int32, (TAPS, TAPS), 0)
        + lax.broadcasted_iota(jnp.int32, (TAPS, TAPS), 1)
        == TAPS - 1
    )
    taps[0] = rounded.astype(F32)
    taps[1] = dot(rounded, flip.astype(F32).astype(BF16), ((1,), (0,)))

    def toeplitz(which, first, out, i):
        eight = taps[which, pl.ds(pl.multiple_of(i * PER, PER), PER), :]
        pieces = []
        for g in range(PER):
            row = jnp.concatenate([eight[g : g + 1], jnp.zeros((1, WIDTH - TAPS), F32)], axis=1)
            wide = jnp.broadcast_to(row, (BLK, WIDTH))
            pieces.append(pltpu.roll(wide, first, 1, stride=1, stride_axis=0).astype(BF16))
        out[i] = jnp.concatenate(pieces, axis=0)

    each(groups // PER, lambda i: toeplitz(0, 0, toep_b, i))

    @pl.when(jnp.logical_not(has_next))
    def _():
        wext[:, rows:, :] = jnp.zeros((n_chunks, rows, chunk), BF16)

    @pl.when(jnp.logical_not(has_prev))
    def _():
        pext[:, :rows, :] = jnp.zeros((n_chunks, rows, chunk), BF16)

    @pl.when(pp == n_pp - 1)
    def _():
        dv[n_chunks] = jnp.zeros((rows, chunk), BF16)

        def clear(i):
            cols = pl.ds(pl.multiple_of(i * chunk, chunk), chunk)
            pltpu.make_async_copy(
                dv.at[n_chunks], ho_hbm.at[0, :, cols], out_sem.at[2, i]).start()
        each(n_chunks, clear)

    pl.semaphore_wait(barrier, n_ctx - 1 + n_quad - 1)

    def send_w(i):
        return pltpu.make_async_remote_copy(
            src_ref=wext.at[i, pl.ds(0, rows)], dst_ref=wext.at[i, pl.ds(rows, rows)],
            send_sem=w_send.at[i], recv_sem=w_recv.at[i],
            device_id={"ctx": ctx - 1}, device_id_type=MESH)

    def send_p(i):
        return pltpu.make_async_remote_copy(
            src_ref=pext.at[i, pl.ds(rows, rows)], dst_ref=pext.at[i, pl.ds(0, rows)],
            send_sem=p_send.at[i], recv_sem=p_recv.at[i],
            device_id={"ctx": ctx + 1}, device_id_type=MESH)

    def send_d(i):
        cols = pl.ds(pl.multiple_of(i * chunk, chunk), chunk)
        return pltpu.make_async_remote_copy(
            src_ref=dv.at[i], dst_ref=ho_hbm.at[0, :, cols],
            send_sem=d_send.at[i], recv_sem=d_recv.at[i],
            device_id={"pp": pp - 1}, device_id_type=MESH)

    def elementwise(i):
        load(0, c_hbm, cv, i).wait()
        load(1, q_hbm, qv, i).wait()
        wext[i, :rows, :] = (cv[i].astype(F32) * qv[i].astype(F32)).astype(BF16)

        @pl.when(has_prev)
        def _():
            send_w(i).start()
        load(2, k_hbm, kv, i).wait()
        load(3, v_hbm, vv, i).wait()
        pext[i, rows:, :] = (kv[i].astype(F32) * vv[i].astype(F32)).astype(BF16)

        @pl.when(has_next)
        def _():
            send_p(i).start()
    each(n_chunks, elementwise)

    owner = lax.broadcasted_iota(jnp.int32, (BLK, LANES), 1) // GROUP

    def filtered(toep, ext, i, s, a):
        mat = toep[i * subs + s, :, :span]
        window = ext[i, a * BLK : a * BLK + span, s * LANES : (s + 1) * LANES]
        full = dot(mat, window, ((1,), (0,)))
        result = full[:BLK]
        for g in range(1, PER):
            result = jnp.where(owner == g, full[g * BLK : (g + 1) * BLK], result)
        return result

    def backward(i):
        @pl.when(has_next)
        def _():
            send_w(i).wait_recv()
        for s in range(subs):
            cols = slice(s * LANES, (s + 1) * LANES)
            for a in range(blocks):
                here = slice(a * BLK, (a + 1) * BLK)
                dprod = filtered(toep_b, wext, i, s, a)
                dv[i, here, cols] = (dprod * kv[i, here, cols].astype(F32)).astype(BF16)
                gk[i, here, cols] = (dprod * vv[i, here, cols].astype(F32)).astype(BF16)

        @pl.when(pp > 0)
        def _():
            send_d(i).start()
        store(0, gk, gk_hbm, i).start()
    each(n_chunks, backward)

    place = lax.broadcasted_iota(jnp.int32, (8, WIDTH), 0)

    def tap_grad(i):
        for s in range(subs):
            cols = slice(s * LANES, (s + 1) * LANES)
            left, right = [], []
            for a in range(blocks):
                own = pext[i, rows + a * BLK : rows + (a + 1) * BLK, cols]
                left.append(jnp.concatenate(
                    [jnp.where(owner == g, own, jnp.zeros_like(own)) for g in range(PER)], axis=0))
                right.append(wext[i, a * BLK : a * BLK + span, cols])
            pairs = dot(
                jnp.concatenate(left, axis=1), jnp.concatenate(right, axis=1), ((1,), (1,)))
            pairs = jnp.concatenate(
                [pairs, jnp.zeros((PER * BLK, WIDTH - span), F32)], axis=1)
            sums = []
            for g in range(PER):
                total = pairs[g * BLK : g * BLK + 8]
                for b in range(8, BLK, 8):
                    total = total + pltpu.roll(
                        pairs[g * BLK + b : g * BLK + b + 8], WIDTH - b, 1)
                for bit in (1, 2, 4):
                    moved = pltpu.roll(total, WIDTH - bit, 1)
                    total = jnp.where((place & bit) != 0, moved, total)
                sums.append(jnp.sum(total[:, :TAPS], axis=0, keepdims=True))
            at = pl.ds(pl.multiple_of((i * subs + s) * PER, PER), PER)
            raws[ctx, at, :] = jnp.concatenate(sums, axis=0)
    each(n_chunks, tap_grad)

    def send_r(d):
        return pltpu.make_async_remote_copy(
            src_ref=raws.at[ctx], dst_ref=raws.at[ctx],
            send_sem=r_send.at[d], recv_sem=r_recv.at[d],
            device_id=ctx_peer(d + 1), device_id_type=MESH)

    def recv_r(d):
        slot = lax.rem(ctx + n_ctx - 1 - d, n_ctx)
        return pltpu.make_async_remote_copy(
            src_ref=raws.at[slot], dst_ref=raws.at[slot],
            send_sem=r_send.at[d], recv_sem=r_recv.at[d],
            device_id=ctx_peer(d + 1), device_id_type=MESH)
    each(n_ctx - 1, lambda d: send_r(d).start())

    each(groups // PER, lambda i: toeplitz(1, 1, toep_f, i))

    def forward(i):
        @pl.when(has_prev)
        def _():
            send_p(i).wait_recv()
        for s in range(subs):
            cols = slice(s * LANES, (s + 1) * LANES)
            for a in range(blocks):
                here = slice(a * BLK, (a + 1) * BLK)
                mixed = filtered(toep_f, pext, i, s, a)
                gq[i, here, cols] = (mixed * cv[i, here, cols].astype(F32)).astype(BF16)
        store(1, gq, gq_hbm, i).start()

    each(n_chunks, forward)

    each(n_ctx - 1, lambda d: recv_r(d).wait_recv())
    summed = raws[0]
    for d in range(1, n_ctx):
        summed = summed + raws[d]
    squares = jnp.sum(summed * summed, axis=0, keepdims=True)
    norms[me] = jnp.broadcast_to(squares, (8, TAPS))

    def send_n(d):
        return pltpu.make_async_remote_copy(
            src_ref=norms.at[me], dst_ref=norms.at[me],
            send_sem=n_send.at[d], recv_sem=n_recv.at[d],
            device_id=quad(d + 1), device_id_type=MESH)

    def recv_n(d):
        slot = lax.rem(me + n_quad - 1 - d, n_quad)
        return pltpu.make_async_remote_copy(
            src_ref=norms.at[slot], dst_ref=norms.at[slot],
            send_sem=n_send.at[d], recv_sem=n_recv.at[d],
            device_id=quad(d + 1), device_id_type=MESH)
    each(n_quad - 1, lambda d: send_n(d).start())
    each(n_quad - 1, lambda d: recv_n(d).wait_recv())
    squares = norms[0]
    for d in range(1, n_quad):
        squares = squares + norms[d]
    norm_sq = jnp.sum(squares[:1], axis=1, keepdims=True)
    factor = jnp.minimum(1.0, clip_level / (jnp.sqrt(norm_sq) + 1e-6))
    gf_ref[0] = summed * factor

    each(n_ctx - 1, lambda d: send_r(d).wait_send())
    each(n_quad - 1, lambda d: send_n(d).wait_send())

    def drain(i):
        store(0, gk, gk_hbm, i).wait()
        store(1, gq, gq_hbm, i).wait()

        @pl.when(has_prev)
        def _():
            send_w(i).wait_send()

        @pl.when(has_next)
        def _():
            send_p(i).wait_send()

        @pl.when(pp > 0)
        def _():
            send_d(i).wait_send()

        @pl.when(pp < n_pp - 1)
        def _():
            send_d(i).wait_recv()

        @pl.when(pp == n_pp - 1)
        def _():
            cols = pl.ds(pl.multiple_of(i * chunk, chunk), chunk)
            pltpu.make_async_copy(
                dv.at[n_chunks], ho_hbm.at[0, :, cols], out_sem.at[2, i]).wait()
    each(n_chunks, drain)


def per_device(sizes, queries, key_feats, value_feats, cotangent, filters):
    n_ctx, n_tp, n_pp = sizes
    _, rows, channels = queries.shape
    groups = filters.shape[1]
    chunk = math.gcd(channels, 256)
    n_chunks = channels // chunk
    n_quad = n_tp * n_pp
    clip_level = 0.25 * math.sqrt(n_pp * n_tp * groups * TAPS)
    block = jax.ShapeDtypeStruct(queries.shape, BF16)
    own = pltpu.VMEM((n_chunks, rows, chunk), BF16)
    double = pltpu.VMEM((n_chunks, 2 * rows, chunk), BF16)
    toep = pltpu.VMEM((groups // PER, PER * BLK, WIDTH), BF16)
    dma = pltpu.SemaphoreType.DMA
    per_chunk = dma((n_chunks,))
    hbm = pl.BlockSpec(memory_space=pl.ANY)
    vmem = pl.BlockSpec(memory_space=pltpu.VMEM)
    return pl.pallas_call(
        functools.partial(kernel, sizes, chunk, clip_level),
        out_shape=(block, block, block, jax.ShapeDtypeStruct(filters.shape, F32)),
        in_specs=[hbm] * 4 + [vmem],
        out_specs=(hbm, hbm, hbm, vmem),
        scratch_shapes=[
            own, own, own, own, double, double, own, own,
            pltpu.VMEM((n_chunks + 1, rows, chunk), BF16),
            toep, toep,
            pltpu.VMEM((2, groups, TAPS), F32),
            pltpu.VMEM((n_ctx, groups, TAPS), F32),
            pltpu.VMEM((n_quad, 8, TAPS), F32),
            dma((4, n_chunks)), dma((3, n_chunks)),
            per_chunk, per_chunk, per_chunk, per_chunk, per_chunk, per_chunk,
            dma((n_ctx,)), dma((n_ctx,)), dma((n_quad,)), dma((n_quad,)),
        ],
        compiler_params=pltpu.CompilerParams(
            collective_id=0, has_side_effects=True, vmem_limit_bytes=48 << 20),
    )(queries, key_feats, value_feats, cotangent, filters)


def solution(mesh):
    sizes = tuple(mesh.shape[a] for a in ("ctx", "tp", "pp"))
    tokens = P("pp", "ctx", "tp")
    taps = P("pp", "tp", None)
    return jax.shard_map(
        functools.partial(per_device, sizes),
        mesh=mesh,
        in_specs=(tokens, tokens, tokens, tokens, taps),
        out_specs=(tokens, tokens, tokens, taps),
        check_vma=False,
    )
```

```python
import functools
import math

import jax
import jax.numpy as jnp
from jax import lax
from jax.experimental import pallas as pl
from jax.experimental.pallas import tpu as pltpu
from jax.sharding import PartitionSpec as P

TAPS = 128
GROUP = 16
LANES = 128
PER = LANES // GROUP
BLK = 32
WIDTH = 256
MESH = pl.DeviceIdType.MESH
F32 = jnp.float32
BF16 = jnp.bfloat16


def dot(lhs, rhs, contract):
    return lax.dot_general(lhs, rhs, (contract, ((), ())), preferred_element_type=F32)


def kernel(
    sizes, chunk, clip_level,
    q_hbm, k_hbm, v_hbm, c_hbm, f_hbm,
    gq, gk, ho, gf_ref,
    qv, kv, vv, cv, fv, wext, pext, dv, toep_b, toep_f, taps, raws, norms,
    in_sem, f_sem, w_send, w_recv, p_send, p_recv, d_send, d_recv,
    r_send, r_recv, n_send, n_recv,
):
    n_ctx, n_tp, n_pp = sizes
    ctx, tp, pp = (lax.axis_index(a) for a in ("ctx", "tp", "pp"))
    n_chunks, rows, _ = qv.shape
    groups = fv.shape[0]
    n_quad = n_tp * n_pp
    me = pp * n_tp + tp
    has_next, has_prev = ctx < n_ctx - 1, ctx > 0
    span = BLK + TAPS
    blocks = rows // BLK
    subs = chunk // LANES

    def each(count, body):
        def step(i, _):
            body(i)
            return 0
        lax.fori_loop(0, count, step, 0)

    def ctx_peer(d):
        return {"ctx": lax.rem(ctx + d, n_ctx)}

    def quad(d):
        other = lax.rem(me + d, n_quad)
        return {"tp": lax.rem(other, n_tp), "pp": other // n_tp}

    barrier = pltpu.get_barrier_semaphore()
    each(n_ctx - 1, lambda d: pl.semaphore_signal(
        barrier, inc=1, device_id=ctx_peer(d + 1), device_id_type=MESH))
    each(n_quad - 1, lambda d: pl.semaphore_signal(
        barrier, inc=1, device_id=quad(d + 1), device_id_type=MESH))

    def load(which, hbm, vmem, i):
        cols = pl.ds(pl.multiple_of(i * chunk, chunk), chunk)
        return pltpu.make_async_copy(hbm.at[0, :, cols], vmem.at[i], in_sem.at[which, i])

    loads = ((c_hbm, cv), (q_hbm, qv), (k_hbm, kv), (v_hbm, vv))

    def start_loads(i):
        for which, (hbm, vmem) in enumerate(loads):
            load(which, hbm, vmem, i).start()
    load_taps = pltpu.make_async_copy(f_hbm.at[0], fv, f_sem)
    load_taps.start()
    each(n_chunks, start_loads)
    load_taps.wait()

    rounded = fv[...].astype(BF16)
    flip = (
        lax.broadcasted_iota(jnp.int32, (TAPS, TAPS), 0)
        + lax.broadcasted_iota(jnp.int32, (TAPS, TAPS), 1)
        == TAPS - 1
    )
    taps[0] = rounded.astype(F32)
    taps[1] = dot(rounded, flip.astype(F32).astype(BF16), ((1,), (0,)))

    def toeplitz(which, first, out, i):
        eight = taps[which, pl.ds(pl.multiple_of(i * PER, PER), PER), :]
        pieces = []
        for g in range(PER):
            row = jnp.concatenate([eight[g : g + 1], jnp.zeros((1, WIDTH - TAPS), F32)], axis=1)
            wide = jnp.broadcast_to(row, (BLK, WIDTH))
            pieces.append(pltpu.roll(wide, first, 1, stride=1, stride_axis=0).astype(BF16))
        out[i] = jnp.concatenate(pieces, axis=0)

    each(groups // PER, lambda i: toeplitz(0, 0, toep_b, i))

    @pl.when(jnp.logical_not(has_next))
    def _():
        wext[:, rows:, :] = jnp.zeros((n_chunks, rows, chunk), BF16)

    @pl.when(jnp.logical_not(has_prev))
    def _():
        pext[:, :rows, :] = jnp.zeros((n_chunks, rows, chunk), BF16)

    @pl.when(pp == n_pp - 1)
    def _():
        ho[...] = jnp.zeros_like(ho)

    pl.semaphore_wait(barrier, n_ctx - 1 + n_quad - 1)

    def send_w(i):
        return pltpu.make_async_remote_copy(
            src_ref=wext.at[i, pl.ds(0, rows)], dst_ref=wext.at[i, pl.ds(rows, rows)],
            send_sem=w_send.at[i], recv_sem=w_recv.at[i],
            device_id={"ctx": ctx - 1}, device_id_type=MESH)

    def send_p(i):
        return pltpu.make_async_remote_copy(
            src_ref=pext.at[i, pl.ds(rows, rows)], dst_ref=pext.at[i, pl.ds(0, rows)],
            send_sem=p_send.at[i], recv_sem=p_recv.at[i],
            device_id={"ctx": ctx + 1}, device_id_type=MESH)

    def send_d(i):
        cols = pl.ds(pl.multiple_of(i * chunk, chunk), chunk)
        return pltpu.make_async_remote_copy(
            src_ref=dv.at[i], dst_ref=ho.at[0, :, cols],
            send_sem=d_send.at[i], recv_sem=d_recv.at[i],
            device_id={"pp": pp - 1}, device_id_type=MESH)

    def elementwise(i):
        load(0, c_hbm, cv, i).wait()
        load(1, q_hbm, qv, i).wait()
        wext[i, :rows, :] = (cv[i].astype(F32) * qv[i].astype(F32)).astype(BF16)

        @pl.when(has_prev)
        def _():
            send_w(i).start()
        load(2, k_hbm, kv, i).wait()
        load(3, v_hbm, vv, i).wait()
        pext[i, rows:, :] = (kv[i].astype(F32) * vv[i].astype(F32)).astype(BF16)

        @pl.when(has_next)
        def _():
            send_p(i).start()
    each(n_chunks, elementwise)

    def lanes_of(i, s):
        return pl.ds(pl.multiple_of(i * chunk + s * LANES, LANES), LANES)

    owner = lax.broadcasted_iota(jnp.int32, (BLK, LANES), 1) // GROUP

    def filtered(toep, ext, i, s, a):
        mat = toep[i * subs + s, :, :span]
        window = ext[i, a * BLK : a * BLK + span, s * LANES : (s + 1) * LANES]
        full = dot(mat, window, ((1,), (0,)))
        result = full[:BLK]
        for g in range(1, PER):
            result = jnp.where(owner == g, full[g * BLK : (g + 1) * BLK], result)
        return result

    def backward(i):
        @pl.when(has_next)
        def _():
            send_w(i).wait_recv()
        for s in range(subs):
            cols = slice(s * LANES, (s + 1) * LANES)
            for a in range(blocks):
                here = slice(a * BLK, (a + 1) * BLK)
                dprod = filtered(toep_b, wext, i, s, a)
                dv[i, here, cols] = (dprod * kv[i, here, cols].astype(F32)).astype(BF16)
                gk[0, here, lanes_of(i, s)] = (dprod * vv[i, here, cols].astype(F32)).astype(BF16)

        @pl.when(pp > 0)
        def _():
            send_d(i).start()
    each(n_chunks, backward)

    place = lax.broadcasted_iota(jnp.int32, (8, WIDTH), 0)

    def tap_grad(i):
        for s in range(subs):
            cols = slice(s * LANES, (s + 1) * LANES)
            left, right = [], []
            for a in range(blocks):
                own = pext[i, rows + a * BLK : rows + (a + 1) * BLK, cols]
                left.append(jnp.concatenate(
                    [jnp.where(owner == g, own, jnp.zeros_like(own)) for g in range(PER)], axis=0))
                right.append(wext[i, a * BLK : a * BLK + span, cols])
            pairs = dot(
                jnp.concatenate(left, axis=1), jnp.concatenate(right, axis=1), ((1,), (1,)))
            pairs = jnp.concatenate(
                [pairs, jnp.zeros((PER * BLK, WIDTH - span), F32)], axis=1)
            sums = []
            for g in range(PER):
                total = pairs[g * BLK : g * BLK + 8]
                for b in range(8, BLK, 8):
                    total = total + pltpu.roll(
                        pairs[g * BLK + b : g * BLK + b + 8], WIDTH - b, 1)
                for bit in (1, 2, 4):
                    moved = pltpu.roll(total, WIDTH - bit, 1)
                    total = jnp.where((place & bit) != 0, moved, total)
                sums.append(jnp.sum(total[:, :TAPS], axis=0, keepdims=True))
            at = pl.ds(pl.multiple_of((i * subs + s) * PER, PER), PER)
            raws[ctx, at, :] = jnp.concatenate(sums, axis=0)
    each(n_chunks, tap_grad)

    def send_r(d):
        return pltpu.make_async_remote_copy(
            src_ref=raws.at[ctx], dst_ref=raws.at[ctx],
            send_sem=r_send.at[d], recv_sem=r_recv.at[d],
            device_id=ctx_peer(d + 1), device_id_type=MESH)

    def recv_r(d):
        slot = lax.rem(ctx + n_ctx - 1 - d, n_ctx)
        return pltpu.make_async_remote_copy(
            src_ref=raws.at[slot], dst_ref=raws.at[slot],
            send_sem=r_send.at[d], recv_sem=r_recv.at[d],
            device_id=ctx_peer(d + 1), device_id_type=MESH)
    each(n_ctx - 1, lambda d: send_r(d).start())

    each(groups // PER, lambda i: toeplitz(1, 1, toep_f, i))

    def forward(i):
        @pl.when(has_prev)
        def _():
            send_p(i).wait_recv()
        for s in range(subs):
            cols = slice(s * LANES, (s + 1) * LANES)
            for a in range(blocks):
                here = slice(a * BLK, (a + 1) * BLK)
                mixed = filtered(toep_f, pext, i, s, a)
                gq[0, here, lanes_of(i, s)] = (mixed * cv[i, here, cols].astype(F32)).astype(BF16)

    each(n_chunks, forward)

    each(n_ctx - 1, lambda d: recv_r(d).wait_recv())
    summed = raws[0]
    for d in range(1, n_ctx):
        summed = summed + raws[d]
    squares = jnp.sum(summed * summed, axis=0, keepdims=True)
    norms[me] = jnp.broadcast_to(squares, (8, TAPS))

    def send_n(d):
        return pltpu.make_async_remote_copy(
            src_ref=norms.at[me], dst_ref=norms.at[me],
            send_sem=n_send.at[d], recv_sem=n_recv.at[d],
            device_id=quad(d + 1), device_id_type=MESH)

    def recv_n(d):
        slot = lax.rem(me + n_quad - 1 - d, n_quad)
        return pltpu.make_async_remote_copy(
            src_ref=norms.at[slot], dst_ref=norms.at[slot],
            send_sem=n_send.at[d], recv_sem=n_recv.at[d],
            device_id=quad(d + 1), device_id_type=MESH)
    each(n_quad - 1, lambda d: send_n(d).start())
    each(n_quad - 1, lambda d: recv_n(d).wait_recv())
    squares = norms[0]
    for d in range(1, n_quad):
        squares = squares + norms[d]
    norm_sq = jnp.sum(squares[:1], axis=1, keepdims=True)
    factor = jnp.minimum(1.0, clip_level / (jnp.sqrt(norm_sq) + 1e-6))
    gf_ref[0] = summed * factor

    each(n_ctx - 1, lambda d: send_r(d).wait_send())
    each(n_quad - 1, lambda d: send_n(d).wait_send())

    def drain(i):
        @pl.when(has_prev)
        def _():
            send_w(i).wait_send()

        @pl.when(has_next)
        def _():
            send_p(i).wait_send()

        @pl.when(pp > 0)
        def _():
            send_d(i).wait_send()

        @pl.when(pp < n_pp - 1)
        def _():
            send_d(i).wait_recv()
    each(n_chunks, drain)


def write_back(*refs):
    n = (len(refs) - 1) // 2
    copies = [
        pltpu.make_async_copy(refs[i], refs[n + i], refs[2 * n].at[i]) for i in range(n)
    ]
    for copy in copies:
        copy.start()
    for copy in copies:
        copy.wait()


def per_device(sizes, queries, key_feats, value_feats, cotangent, filters):
    n_ctx, n_tp, n_pp = sizes
    _, rows, channels = queries.shape
    groups = filters.shape[1]
    chunk = math.gcd(channels, 256)
    n_chunks = channels // chunk
    n_quad = n_tp * n_pp
    clip_level = 0.25 * math.sqrt(n_pp * n_tp * groups * TAPS)
    block = jax.ShapeDtypeStruct(queries.shape, BF16)
    own = pltpu.VMEM((n_chunks, rows, chunk), BF16)
    double = pltpu.VMEM((n_chunks, 2 * rows, chunk), BF16)
    toep = pltpu.VMEM((groups // PER, PER * BLK, WIDTH), BF16)
    dma = pltpu.SemaphoreType.DMA
    per_chunk = dma((n_chunks,))
    hbm = pl.BlockSpec(memory_space=pltpu.HBM)
    vmem = pl.BlockSpec(memory_space=pltpu.VMEM)
    out_shape = (block, block, block, jax.ShapeDtypeStruct(filters.shape, F32))
    results = pl.pallas_call(
        functools.partial(kernel, sizes, chunk, clip_level),
        out_shape=out_shape,
        in_specs=[hbm] * 5,
        out_specs=(vmem,) * 4,
        scratch_shapes=[
            own, own, own, own, pltpu.VMEM((groups, TAPS), F32), double, double, own,
            toep, toep,
            pltpu.VMEM((2, groups, TAPS), F32),
            pltpu.VMEM((n_ctx, groups, TAPS), F32),
            pltpu.VMEM((n_quad, 8, TAPS), F32),
            dma((4, n_chunks)), dma,
            per_chunk, per_chunk, per_chunk, per_chunk, per_chunk, per_chunk,
            dma((n_ctx,)), dma((n_ctx,)), dma((n_quad,)), dma((n_quad,)),
        ],
        compiler_params=pltpu.CompilerParams(
            collective_id=0, has_side_effects=True, vmem_limit_bytes=48 << 20),
    )(*[pltpu.with_memory_space_constraint(x, pltpu.HBM) for x in (queries, key_feats, value_feats, cotangent, filters)])
    return pl.pallas_call(
        write_back,
        out_shape=out_shape,
        in_specs=[pl.BlockSpec(memory_space=pl.ANY)] * 4,
        out_specs=(hbm,) * 4,
        scratch_shapes=[dma((4,))],
        compiler_params=pltpu.CompilerParams(vmem_limit_bytes=16 << 20),
    )(*results)


def solution(mesh):
    sizes = tuple(mesh.shape[a] for a in ("ctx", "tp", "pp"))
    tokens = P("pp", "ctx", "tp")
    taps = P("pp", "tp", None)
    return jax.shard_map(
        functools.partial(per_device, sizes),
        mesh=mesh,
        in_specs=(tokens, tokens, tokens, tokens, taps),
        out_specs=(tokens, tokens, tokens, taps),
        check_vma=False,
    )
```

```python
import functools
import math

import jax
import jax.numpy as jnp
from jax import lax
from jax.experimental import pallas as pl
from jax.experimental.pallas import tpu as pltpu
from jax.sharding import PartitionSpec as P

TAPS = 128
GROUP = 16
LANES = 128
PER = LANES // GROUP
BLK = 32
TBLK = 16
WIDTH = 256
MESH = pl.DeviceIdType.MESH
F32 = jnp.float32
BF16 = jnp.bfloat16


def dot(lhs, rhs, contract):
    return lax.dot_general(lhs, rhs, (contract, ((), ())), preferred_element_type=F32)


def kernel(
    sizes, chunk, clip_level,
    q_hbm, k_hbm, v_hbm, c_hbm, f_hbm,
    gq, gk, ho, gf_ref,
    qv, kv, vv, cv, fv, wext, pext, dv, toep_b, toep_f, taps, raws, total, norms,
    in_sem, f_sem, w_send, w_recv, p_send, p_recv, d_send, d_recv,
    r_send, r_recv, n_send, n_recv,
):
    n_ctx, n_tp, n_pp = sizes
    ctx, tp, pp = (lax.axis_index(a) for a in ("ctx", "tp", "pp"))
    n_chunks, rows, _ = qv.shape
    groups = fv.shape[0]
    n_quad = n_tp * n_pp
    me = pp * n_tp + tp
    has_next, has_prev = ctx < n_ctx - 1, ctx > 0
    span = BLK + TAPS
    blocks = rows // BLK
    subs = chunk // LANES

    def each(count, body):
        def step(i, _):
            body(i)
            return 0
        lax.fori_loop(0, count, step, 0)

    def ctx_peer(d):
        return {"ctx": lax.rem(ctx + d, n_ctx)}

    def quad(d):
        other = lax.rem(me + d, n_quad)
        return {"tp": lax.rem(other, n_tp), "pp": other // n_tp}

    barrier = pltpu.get_barrier_semaphore()
    each(n_ctx - 1, lambda d: pl.semaphore_signal(
        barrier, inc=1, device_id=ctx_peer(d + 1), device_id_type=MESH))
    each(n_quad - 1, lambda d: pl.semaphore_signal(
        barrier, inc=1, device_id=quad(d + 1), device_id_type=MESH))

    def load(which, hbm, vmem, i):
        cols = pl.ds(pl.multiple_of(i * chunk, chunk), chunk)
        return pltpu.make_async_copy(hbm.at[0, :, cols], vmem.at[i], in_sem.at[which, i])

    loads = ((c_hbm, cv), (q_hbm, qv), (k_hbm, kv), (v_hbm, vv))

    def start_loads(i):
        for which, (hbm, vmem) in enumerate(loads):
            load(which, hbm, vmem, i).start()
    load_taps = pltpu.make_async_copy(f_hbm.at[0], fv, f_sem)
    load_taps.start()
    each(n_chunks, start_loads)
    load_taps.wait()

    rounded = fv[...].astype(BF16)
    flip = (
        lax.broadcasted_iota(jnp.int32, (TAPS, TAPS), 0)
        + lax.broadcasted_iota(jnp.int32, (TAPS, TAPS), 1)
        == TAPS - 1
    )
    taps[0] = rounded.astype(F32)
    taps[1] = dot(rounded, flip.astype(F32).astype(BF16), ((1,), (0,)))

    def toeplitz(which, first, out, i):
        eight = taps[which, pl.ds(pl.multiple_of(i * PER, PER), PER), :]
        pieces = []
        for g in range(PER):
            row = jnp.concatenate([eight[g : g + 1], jnp.zeros((1, WIDTH - TAPS), F32)], axis=1)
            wide = jnp.broadcast_to(row, (BLK, WIDTH))
            pieces.append(pltpu.roll(wide, first, 1, stride=1, stride_axis=0).astype(BF16))
        out[i] = jnp.concatenate(pieces, axis=0)

    each(groups // PER, lambda i: toeplitz(0, 0, toep_b, i))

    @pl.when(jnp.logical_not(has_next))
    def _():
        wext[:, rows:, :] = jnp.zeros((n_chunks, rows, chunk), BF16)

    @pl.when(jnp.logical_not(has_prev))
    def _():
        pext[:, :rows, :] = jnp.zeros((n_chunks, rows, chunk), BF16)

    @pl.when(pp == n_pp - 1)
    def _():
        ho[...] = jnp.zeros_like(ho)

    pl.semaphore_wait(barrier, n_ctx - 1 + n_quad - 1)

    def send_w(i):
        return pltpu.make_async_remote_copy(
            src_ref=wext.at[i, pl.ds(0, rows)], dst_ref=wext.at[i, pl.ds(rows, rows)],
            send_sem=w_send.at[i], recv_sem=w_recv.at[i],
            device_id={"ctx": ctx - 1}, device_id_type=MESH)

    def send_p(i):
        return pltpu.make_async_remote_copy(
            src_ref=pext.at[i, pl.ds(rows, rows)], dst_ref=pext.at[i, pl.ds(0, rows)],
            send_sem=p_send.at[i], recv_sem=p_recv.at[i],
            device_id={"ctx": ctx + 1}, device_id_type=MESH)

    def send_d(i):
        cols = pl.ds(pl.multiple_of(i * chunk, chunk), chunk)
        return pltpu.make_async_remote_copy(
            src_ref=dv.at[i], dst_ref=ho.at[0, :, cols],
            send_sem=d_send.at[i], recv_sem=d_recv.at[i],
            device_id={"pp": pp - 1}, device_id_type=MESH)

    def elementwise(i):
        load(0, c_hbm, cv, i).wait()
        load(1, q_hbm, qv, i).wait()
        wext[i, :rows, :] = (cv[i].astype(F32) * qv[i].astype(F32)).astype(BF16)

        @pl.when(has_prev)
        def _():
            send_w(i).start()
        load(2, k_hbm, kv, i).wait()
        load(3, v_hbm, vv, i).wait()
        pext[i, rows:, :] = (kv[i].astype(F32) * vv[i].astype(F32)).astype(BF16)

        @pl.when(has_next)
        def _():
            send_p(i).start()
    each(n_chunks, elementwise)
    each(groups // PER, lambda i: toeplitz(1, 1, toep_f, i))

    def lanes_of(i, s):
        return pl.ds(pl.multiple_of(i * chunk + s * LANES, LANES), LANES)

    owner = lax.broadcasted_iota(jnp.int32, (BLK, LANES), 1) // GROUP

    def filtered(toep, ext, i, s, a):
        mat = toep[i * subs + s, :, :span]
        window = ext[i, a * BLK : a * BLK + span, s * LANES : (s + 1) * LANES]
        full = dot(mat, window, ((1,), (0,)))
        result = full[:BLK]
        for g in range(1, PER):
            result = jnp.where(owner == g, full[g * BLK : (g + 1) * BLK], result)
        return result

    def backward(i):
        @pl.when(has_next)
        def _():
            send_w(i).wait_recv()
        for s in range(subs):
            cols = slice(s * LANES, (s + 1) * LANES)
            for a in range(blocks):
                here = slice(a * BLK, (a + 1) * BLK)
                dprod = filtered(toep_b, wext, i, s, a)
                dv[i, here, cols] = (dprod * kv[i, here, cols].astype(F32)).astype(BF16)
                gk[0, here, lanes_of(i, s)] = (dprod * vv[i, here, cols].astype(F32)).astype(BF16)

        @pl.when(pp > 0)
        def _():
            send_d(i).start()

    place = lax.broadcasted_iota(jnp.int32, (8, WIDTH), 0)

    own_taps = owner[:TBLK]

    def tap_grad(i):
        for s in range(subs):
            cols = slice(s * LANES, (s + 1) * LANES)
            left, right = [], []
            for a in range(rows // TBLK):
                own = pext[i, rows + a * TBLK : rows + (a + 1) * TBLK, cols]
                left.append(jnp.concatenate(
                    [jnp.where(own_taps == g, own, jnp.zeros_like(own)) for g in range(PER)], axis=0))
                right.append(wext[i, a * TBLK : a * TBLK + TBLK + TAPS, cols])
            pairs = dot(
                jnp.concatenate(left, axis=1), jnp.concatenate(right, axis=1), ((1,), (1,)))
            pairs = jnp.concatenate(
                [pairs, jnp.zeros((PER * TBLK, WIDTH - TBLK - TAPS), F32)], axis=1)
            sums = []
            for g in range(PER):
                partial = pairs[g * TBLK : g * TBLK + 8]
                for b in range(8, TBLK, 8):
                    partial = partial + pltpu.roll(
                        pairs[g * TBLK + b : g * TBLK + b + 8], WIDTH - b, 1)
                for bit in (1, 2, 4):
                    moved = pltpu.roll(partial, WIDTH - bit, 1)
                    partial = jnp.where((place & bit) != 0, moved, partial)
                sums.append(jnp.sum(partial[:, :TAPS], axis=0, keepdims=True))
            at = pl.ds(pl.multiple_of((i * subs + s) * PER, PER), PER)
            raws[ctx, at, :] = jnp.concatenate(sums, axis=0)

    def share(d, slot, i):
        part = raws.at[slot, pl.ds(pl.multiple_of(i * subs * PER, PER), subs * PER)]
        return pltpu.make_async_remote_copy(
            src_ref=part, dst_ref=part,
            send_sem=r_send.at[d, i], recv_sem=r_recv.at[d, i],
            device_id=ctx_peer(d + 1), device_id_type=MESH)

    def send_r(d, i):
        return share(d, ctx, i)

    def recv_r(d, i):
        return share(d, lax.rem(ctx + n_ctx - 1 - d, n_ctx), i)

    def steps(i):
        backward(i)
        tap_grad(i)
        each(n_ctx - 1, lambda d: send_r(d, i).start())
    each(n_chunks, steps)

    def forward(i):
        @pl.when(has_prev)
        def _():
            send_p(i).wait_recv()
        for s in range(subs):
            cols = slice(s * LANES, (s + 1) * LANES)
            for a in range(blocks):
                here = slice(a * BLK, (a + 1) * BLK)
                mixed = filtered(toep_f, pext, i, s, a)
                gq[0, here, lanes_of(i, s)] = (mixed * cv[i, here, cols].astype(F32)).astype(BF16)

    early = n_chunks // 2
    each(early, forward)

    each(n_chunks, lambda i: each(n_ctx - 1, lambda d: recv_r(d, i).wait_recv()))
    summed = raws[0]
    for d in range(1, n_ctx):
        summed = summed + raws[d]
    total[...] = summed
    squares = jnp.sum(summed * summed, axis=0, keepdims=True)
    norms[me] = jnp.broadcast_to(squares, (8, TAPS))

    def send_n(d):
        return pltpu.make_async_remote_copy(
            src_ref=norms.at[me], dst_ref=norms.at[me],
            send_sem=n_send.at[d], recv_sem=n_recv.at[d],
            device_id=quad(d + 1), device_id_type=MESH)

    def recv_n(d):
        slot = lax.rem(me + n_quad - 1 - d, n_quad)
        return pltpu.make_async_remote_copy(
            src_ref=norms.at[slot], dst_ref=norms.at[slot],
            send_sem=n_send.at[d], recv_sem=n_recv.at[d],
            device_id=quad(d + 1), device_id_type=MESH)
    each(n_quad - 1, lambda d: send_n(d).start())
    each(n_chunks - early, lambda i: forward(early + i))
    each(n_quad - 1, lambda d: recv_n(d).wait_recv())
    squares = norms[0]
    for d in range(1, n_quad):
        squares = squares + norms[d]
    norm_sq = jnp.sum(squares[:1], axis=1, keepdims=True)
    factor = jnp.minimum(1.0, clip_level / (jnp.sqrt(norm_sq) + 1e-6))
    gf_ref[0] = total[...] * factor

    each(n_chunks, lambda i: each(n_ctx - 1, lambda d: send_r(d, i).wait_send()))
    each(n_quad - 1, lambda d: send_n(d).wait_send())

    def drain(i):
        @pl.when(has_prev)
        def _():
            send_w(i).wait_send()

        @pl.when(has_next)
        def _():
            send_p(i).wait_send()

        @pl.when(pp > 0)
        def _():
            send_d(i).wait_send()

        @pl.when(pp < n_pp - 1)
        def _():
            send_d(i).wait_recv()
    each(n_chunks, drain)


def write_back(*refs):
    n = (len(refs) - 1) // 2
    copies = [
        pltpu.make_async_copy(refs[i], refs[n + i], refs[2 * n].at[i]) for i in range(n)
    ]
    for copy in copies:
        copy.start()
    for copy in copies:
        copy.wait()


def per_device(sizes, queries, key_feats, value_feats, cotangent, filters):
    n_ctx, n_tp, n_pp = sizes
    _, rows, channels = queries.shape
    groups = filters.shape[1]
    chunk = math.gcd(channels, 256)
    n_chunks = channels // chunk
    n_quad = n_tp * n_pp
    clip_level = 0.25 * math.sqrt(n_pp * n_tp * groups * TAPS)
    block = jax.ShapeDtypeStruct(queries.shape, BF16)
    own = pltpu.VMEM((n_chunks, rows, chunk), BF16)
    double = pltpu.VMEM((n_chunks, 2 * rows, chunk), BF16)
    toep = pltpu.VMEM((groups // PER, PER * BLK, WIDTH), BF16)
    dma = pltpu.SemaphoreType.DMA
    per_chunk = dma((n_chunks,))
    hbm = pl.BlockSpec(memory_space=pltpu.HBM)
    vmem = pl.BlockSpec(memory_space=pltpu.VMEM)
    out_shape = (block, block, block, jax.ShapeDtypeStruct(filters.shape, F32))
    results = pl.pallas_call(
        functools.partial(kernel, sizes, chunk, clip_level),
        out_shape=out_shape,
        in_specs=[hbm] * 5,
        out_specs=(vmem,) * 4,
        scratch_shapes=[
            own, own, own, own, pltpu.VMEM((groups, TAPS), F32), double, double, own,
            toep, toep,
            pltpu.VMEM((2, groups, TAPS), F32),
            pltpu.VMEM((n_ctx, groups, TAPS), F32),
            pltpu.VMEM((groups, TAPS), F32),
            pltpu.VMEM((n_quad, 8, TAPS), F32),
            dma((4, n_chunks)), dma,
            per_chunk, per_chunk, per_chunk, per_chunk, per_chunk, per_chunk,
            dma((n_ctx, n_chunks)), dma((n_ctx, n_chunks)), dma((n_quad,)), dma((n_quad,)),
        ],
        compiler_params=pltpu.CompilerParams(
            collective_id=0, has_side_effects=True, vmem_limit_bytes=48 << 20),
    )(*[pltpu.with_memory_space_constraint(x, pltpu.HBM) for x in (queries, key_feats, value_feats, cotangent, filters)])
    return pl.pallas_call(
        write_back,
        out_shape=out_shape,
        in_specs=[pl.BlockSpec(memory_space=pl.ANY)] * 4,
        out_specs=(hbm,) * 4,
        scratch_shapes=[dma((4,))],
        compiler_params=pltpu.CompilerParams(vmem_limit_bytes=16 << 20),
    )(*results)


def solution(mesh):
    sizes = tuple(mesh.shape[a] for a in ("ctx", "tp", "pp"))
    tokens = P("pp", "ctx", "tp")
    taps = P("pp", "tp", None)
    return jax.shard_map(
        functools.partial(per_device, sizes),
        mesh=mesh,
        in_specs=(tokens, tokens, tokens, tokens, taps),
        out_specs=(tokens, tokens, tokens, taps),
        check_vma=False,
    )
```

```python
import functools
import math

import jax
import jax.numpy as jnp
from jax import lax
from jax.experimental import pallas as pl
from jax.experimental.pallas import tpu as pltpu
from jax.sharding import PartitionSpec as P

TAPS = 128
GROUP = 16
LANES = 128
PER = LANES // GROUP
BLK = 16
TBLK = 16
WIDTH = 256
MESH = pl.DeviceIdType.MESH
F32 = jnp.float32
BF16 = jnp.bfloat16


def dot(lhs, rhs, contract):
    return lax.dot_general(lhs, rhs, (contract, ((), ())), preferred_element_type=F32)


def kernel(
    sizes, chunk, clip_level,
    q_hbm, k_hbm, v_hbm, c_hbm, f_hbm,
    gq, gk, ho, gf_ref,
    qv, kv, vv, cv, fv, wext, pext, dv, toep_b, toep_f, taps, raws, total, norms,
    in_sem, f_sem, w_send, w_recv, p_send, p_recv, d_send, d_recv,
    r_send, r_recv, n_send, n_recv,
):
    n_ctx, n_tp, n_pp = sizes
    ctx, tp, pp = (lax.axis_index(a) for a in ("ctx", "tp", "pp"))
    n_chunks, rows, _ = qv.shape
    groups = fv.shape[0]
    n_quad = n_tp * n_pp
    me = pp * n_tp + tp
    has_next, has_prev = ctx < n_ctx - 1, ctx > 0
    span = BLK + TAPS
    blocks = rows // BLK
    subs = chunk // LANES

    def each(count, body):
        def step(i, _):
            body(i)
            return 0
        lax.fori_loop(0, count, step, 0)

    def ctx_peer(d):
        return {"ctx": lax.rem(ctx + d, n_ctx)}

    def quad(d):
        other = lax.rem(me + d, n_quad)
        return {"tp": lax.rem(other, n_tp), "pp": other // n_tp}

    barrier = pltpu.get_barrier_semaphore()
    each(n_ctx - 1, lambda d: pl.semaphore_signal(
        barrier, inc=1, device_id=ctx_peer(d + 1), device_id_type=MESH))
    each(n_quad - 1, lambda d: pl.semaphore_signal(
        barrier, inc=1, device_id=quad(d + 1), device_id_type=MESH))

    def load(which, hbm, vmem, i):
        cols = pl.ds(pl.multiple_of(i * chunk, chunk), chunk)
        return pltpu.make_async_copy(hbm.at[0, :, cols], vmem.at[i], in_sem.at[which, i])

    loads = ((c_hbm, cv), (q_hbm, qv), (k_hbm, kv), (v_hbm, vv))

    def start_loads(i):
        for which, (hbm, vmem) in enumerate(loads):
            load(which, hbm, vmem, i).start()
    load_taps = pltpu.make_async_copy(f_hbm.at[0], fv, f_sem)
    load_taps.start()
    each(n_chunks, start_loads)
    load_taps.wait()

    rounded = fv[...].astype(BF16)
    flip = (
        lax.broadcasted_iota(jnp.int32, (TAPS, TAPS), 0)
        + lax.broadcasted_iota(jnp.int32, (TAPS, TAPS), 1)
        == TAPS - 1
    )
    taps[0] = rounded.astype(F32)
    taps[1] = dot(rounded, flip.astype(F32).astype(BF16), ((1,), (0,)))

    def toeplitz(which, first, out, i):
        eight = taps[which, pl.ds(pl.multiple_of(i * PER, PER), PER), :]
        pieces = []
        for g in range(PER):
            row = jnp.concatenate([eight[g : g + 1], jnp.zeros((1, WIDTH - TAPS), F32)], axis=1)
            wide = jnp.broadcast_to(row, (BLK, WIDTH))
            pieces.append(pltpu.roll(wide, first, 1, stride=1, stride_axis=0).astype(BF16))
        out[i] = jnp.concatenate(pieces, axis=0)

    each(groups // PER, lambda i: toeplitz(0, 0, toep_b, i))

    @pl.when(jnp.logical_not(has_next))
    def _():
        wext[:, rows:, :] = jnp.zeros((n_chunks, rows, chunk), BF16)

    @pl.when(jnp.logical_not(has_prev))
    def _():
        pext[:, :rows, :] = jnp.zeros((n_chunks, rows, chunk), BF16)

    @pl.when(pp == n_pp - 1)
    def _():
        ho[...] = jnp.zeros_like(ho)

    pl.semaphore_wait(barrier, n_ctx - 1 + n_quad - 1)

    def send_w(i):
        return pltpu.make_async_remote_copy(
            src_ref=wext.at[i, pl.ds(0, rows)], dst_ref=wext.at[i, pl.ds(rows, rows)],
            send_sem=w_send.at[i], recv_sem=w_recv.at[i],
            device_id={"ctx": ctx - 1}, device_id_type=MESH)

    def send_p(i):
        return pltpu.make_async_remote_copy(
            src_ref=pext.at[i, pl.ds(rows, rows)], dst_ref=pext.at[i, pl.ds(0, rows)],
            send_sem=p_send.at[i], recv_sem=p_recv.at[i],
            device_id={"ctx": ctx + 1}, device_id_type=MESH)

    def send_d(i):
        cols = pl.ds(pl.multiple_of(i * chunk, chunk), chunk)
        return pltpu.make_async_remote_copy(
            src_ref=dv.at[i], dst_ref=ho.at[0, :, cols],
            send_sem=d_send.at[i], recv_sem=d_recv.at[i],
            device_id={"pp": pp - 1}, device_id_type=MESH)

    def elementwise(i):
        load(0, c_hbm, cv, i).wait()
        load(1, q_hbm, qv, i).wait()
        wext[i, :rows, :] = (cv[i].astype(F32) * qv[i].astype(F32)).astype(BF16)

        @pl.when(has_prev)
        def _():
            send_w(i).start()
        load(2, k_hbm, kv, i).wait()
        load(3, v_hbm, vv, i).wait()
        pext[i, rows:, :] = (kv[i].astype(F32) * vv[i].astype(F32)).astype(BF16)

        @pl.when(has_next)
        def _():
            send_p(i).start()
    each(n_chunks, elementwise)
    each(groups // PER, lambda i: toeplitz(1, 1, toep_f, i))

    def lanes_of(i, s):
        return pl.ds(pl.multiple_of(i * chunk + s * LANES, LANES), LANES)

    owner = lax.broadcasted_iota(jnp.int32, (BLK, LANES), 1) // GROUP

    def filtered(toep, ext, i, s, a):
        mat = toep[i * subs + s, :, :span]
        window = ext[i, a * BLK : a * BLK + span, s * LANES : (s + 1) * LANES]
        full = dot(mat, window, ((1,), (0,)))
        result = full[:BLK]
        for g in range(1, PER):
            result = jnp.where(owner == g, full[g * BLK : (g + 1) * BLK], result)
        return result

    def backward(i):
        @pl.when(has_next)
        def _():
            send_w(i).wait_recv()
        for s in range(subs):
            cols = slice(s * LANES, (s + 1) * LANES)
            for a in range(blocks):
                here = slice(a * BLK, (a + 1) * BLK)
                dprod = filtered(toep_b, wext, i, s, a)
                dv[i, here, cols] = (dprod * kv[i, here, cols].astype(F32)).astype(BF16)
                gk[0, here, lanes_of(i, s)] = (dprod * vv[i, here, cols].astype(F32)).astype(BF16)

        @pl.when(pp > 0)
        def _():
            send_d(i).start()

    place = lax.broadcasted_iota(jnp.int32, (8, WIDTH), 0)

    own_taps = owner[:TBLK]

    def tap_grad(i):
        for s in range(subs):
            cols = slice(s * LANES, (s + 1) * LANES)
            left, right = [], []
            for a in range(rows // TBLK):
                own = pext[i, rows + a * TBLK : rows + (a + 1) * TBLK, cols]
                left.append(jnp.concatenate(
                    [jnp.where(own_taps == g, own, jnp.zeros_like(own)) for g in range(PER)], axis=0))
                right.append(wext[i, a * TBLK : a * TBLK + TBLK + TAPS, cols])
            pairs = dot(
                jnp.concatenate(left, axis=1), jnp.concatenate(right, axis=1), ((1,), (1,)))
            pairs = jnp.concatenate(
                [pairs, jnp.zeros((PER * TBLK, WIDTH - TBLK - TAPS), F32)], axis=1)
            sums = []
            for g in range(PER):
                partial = pairs[g * TBLK : g * TBLK + 8]
                for b in range(8, TBLK, 8):
                    partial = partial + pltpu.roll(
                        pairs[g * TBLK + b : g * TBLK + b + 8], WIDTH - b, 1)
                for bit in (1, 2, 4):
                    moved = pltpu.roll(partial, WIDTH - bit, 1)
                    partial = jnp.where((place & bit) != 0, moved, partial)
                sums.append(jnp.sum(partial[:, :TAPS], axis=0, keepdims=True))
            at = pl.ds(pl.multiple_of((i * subs + s) * PER, PER), PER)
            raws[ctx, at, :] = jnp.concatenate(sums, axis=0)

    def share(d, slot, i):
        part = raws.at[slot, pl.ds(pl.multiple_of(i * subs * PER, PER), subs * PER)]
        return pltpu.make_async_remote_copy(
            src_ref=part, dst_ref=part,
            send_sem=r_send.at[d, i], recv_sem=r_recv.at[d, i],
            device_id=ctx_peer(d + 1), device_id_type=MESH)

    def send_r(d, i):
        return share(d, ctx, i)

    def recv_r(d, i):
        return share(d, lax.rem(ctx + n_ctx - 1 - d, n_ctx), i)

    def steps(i):
        backward(i)
        tap_grad(i)
        each(n_ctx - 1, lambda d: send_r(d, i).start())
    each(n_chunks, steps)

    def forward(i):
        @pl.when(has_prev)
        def _():
            send_p(i).wait_recv()
        for s in range(subs):
            cols = slice(s * LANES, (s + 1) * LANES)
            for a in range(blocks):
                here = slice(a * BLK, (a + 1) * BLK)
                mixed = filtered(toep_f, pext, i, s, a)
                gq[0, here, lanes_of(i, s)] = (mixed * cv[i, here, cols].astype(F32)).astype(BF16)

    early = n_chunks // 2
    each(early, forward)

    each(n_chunks, lambda i: each(n_ctx - 1, lambda d: recv_r(d, i).wait_recv()))
    summed = raws[0]
    for d in range(1, n_ctx):
        summed = summed + raws[d]
    total[...] = summed
    squares = jnp.sum(summed * summed, axis=0, keepdims=True)
    norms[me] = jnp.broadcast_to(squares, (8, TAPS))

    def send_n(d):
        return pltpu.make_async_remote_copy(
            src_ref=norms.at[me], dst_ref=norms.at[me],
            send_sem=n_send.at[d], recv_sem=n_recv.at[d],
            device_id=quad(d + 1), device_id_type=MESH)

    def recv_n(d):
        slot = lax.rem(me + n_quad - 1 - d, n_quad)
        return pltpu.make_async_remote_copy(
            src_ref=norms.at[slot], dst_ref=norms.at[slot],
            send_sem=n_send.at[d], recv_sem=n_recv.at[d],
            device_id=quad(d + 1), device_id_type=MESH)
    each(n_quad - 1, lambda d: send_n(d).start())
    each(n_chunks - early, lambda i: forward(early + i))
    each(n_quad - 1, lambda d: recv_n(d).wait_recv())
    squares = norms[0]
    for d in range(1, n_quad):
        squares = squares + norms[d]
    norm_sq = jnp.sum(squares[:1], axis=1, keepdims=True)
    factor = jnp.minimum(1.0, clip_level / (jnp.sqrt(norm_sq) + 1e-6))
    gf_ref[0] = total[...] * factor

    each(n_chunks, lambda i: each(n_ctx - 1, lambda d: send_r(d, i).wait_send()))
    each(n_quad - 1, lambda d: send_n(d).wait_send())

    def drain(i):
        @pl.when(has_prev)
        def _():
            send_w(i).wait_send()

        @pl.when(has_next)
        def _():
            send_p(i).wait_send()

        @pl.when(pp > 0)
        def _():
            send_d(i).wait_send()

        @pl.when(pp < n_pp - 1)
        def _():
            send_d(i).wait_recv()
    each(n_chunks, drain)


def write_back(*refs):
    n = (len(refs) - 1) // 2
    copies = [
        pltpu.make_async_copy(refs[i], refs[n + i], refs[2 * n].at[i]) for i in range(n)
    ]
    for copy in copies:
        copy.start()
    for copy in copies:
        copy.wait()


def per_device(sizes, queries, key_feats, value_feats, cotangent, filters):
    n_ctx, n_tp, n_pp = sizes
    _, rows, channels = queries.shape
    groups = filters.shape[1]
    chunk = math.gcd(channels, 512)
    n_chunks = channels // chunk
    n_quad = n_tp * n_pp
    clip_level = 0.25 * math.sqrt(n_pp * n_tp * groups * TAPS)
    block = jax.ShapeDtypeStruct(queries.shape, BF16)
    own = pltpu.VMEM((n_chunks, rows, chunk), BF16)
    double = pltpu.VMEM((n_chunks, 2 * rows, chunk), BF16)
    toep = pltpu.VMEM((groups // PER, PER * BLK, WIDTH), BF16)
    dma = pltpu.SemaphoreType.DMA
    per_chunk = dma((n_chunks,))
    hbm = pl.BlockSpec(memory_space=pltpu.HBM)
    vmem = pl.BlockSpec(memory_space=pltpu.VMEM)
    out_shape = (block, block, block, jax.ShapeDtypeStruct(filters.shape, F32))
    results = pl.pallas_call(
        functools.partial(kernel, sizes, chunk, clip_level),
        out_shape=out_shape,
        in_specs=[hbm] * 5,
        out_specs=(vmem,) * 4,
        scratch_shapes=[
            own, own, own, own, pltpu.VMEM((groups, TAPS), F32), double, double, own,
            toep, toep,
            pltpu.VMEM((2, groups, TAPS), F32),
            pltpu.VMEM((n_ctx, groups, TAPS), F32),
            pltpu.VMEM((groups, TAPS), F32),
            pltpu.VMEM((n_quad, 8, TAPS), F32),
            dma((4, n_chunks)), dma,
            per_chunk, per_chunk, per_chunk, per_chunk, per_chunk, per_chunk,
            dma((n_ctx, n_chunks)), dma((n_ctx, n_chunks)), dma((n_quad,)), dma((n_quad,)),
        ],
        compiler_params=pltpu.CompilerParams(
            collective_id=0, has_side_effects=True, vmem_limit_bytes=48 << 20),
    )(*[pltpu.with_memory_space_constraint(x, pltpu.HBM) for x in (queries, key_feats, value_feats, cotangent, filters)])
    return pl.pallas_call(
        write_back,
        out_shape=out_shape,
        in_specs=[pl.BlockSpec(memory_space=pl.ANY)] * 4,
        out_specs=(hbm,) * 4,
        scratch_shapes=[dma((4,))],
        compiler_params=pltpu.CompilerParams(vmem_limit_bytes=16 << 20),
    )(*results)


def solution(mesh):
    sizes = tuple(mesh.shape[a] for a in ("ctx", "tp", "pp"))
    tokens = P("pp", "ctx", "tp")
    taps = P("pp", "tp", None)
    return jax.shard_map(
        functools.partial(per_device, sizes),
        mesh=mesh,
        in_specs=(tokens, tokens, tokens, tokens, taps),
        out_specs=(tokens, tokens, tokens, taps),
        check_vma=False,
    )
```
